32 devices in a mesh: dp: 2 (over x), expert: 8 (over z, core), tensor: 2 (over y).
Axes of the slice: x: 2, y: 2, z: 4, core: 2. Of those that a mesh axis runs over, the one named last changes fastest.
Arguments:
- tokens: bfloat16 [256, 2048], P(('dp', 'expert')), may hold values from -6 to 6
- routes: int32 [256, 8], P(('dp', 'expert')), may hold values from 0 to 15, all different within a row; in each aligned block of 16 rows (0 to 15, 16 to 31, ...) at most 16 rows name the same one
- route_weight: float32 [256, 8], P(('dp', 'expert')), may hold values from 0.02 to 0.5
- weights_gate_up: bfloat16 [16, 2048, 2, 768], P('expert', None, None, 'tensor'), may hold values from -0.125 to 0.125
- weights_down: bfloat16 [16, 2048, 768], P('expert', None, 'tensor'), may hold values from -0.21875 to 0.21875
- cotangent: bfloat16 [256, 2048], P(('dp', 'expert')), may hold values from -6 to 6
Outputs:
- layer_out: bfloat16 [256, 2048], P(('dp', 'expert'), 'tensor')
- tokens_grad: bfloat16 [256, 2048], P(('dp', 'expert'), 'tensor')
- gate_up_grad: bfloat16 [16, 2048, 2, 768], P('expert', 'dp', None, 'tensor')
- down_grad: bfloat16 [16, 2048, 768], P('expert', 'dp', 'tensor')
The draws below stay inside these ranges and needn't reach their ends.
Inputs may be any that keep to these rules, and one draw needn't show every extreme that they name: `routes`: each row names 8 different experts. Among the 16 rows of one index of dp and expert no expert is named more than 16 times, a bound that some block reaches.
All inputs are finite; a program needn't handle non-finite values.
Results may differ from the reference program's by a relative error of at most 0.0072.
Values may be sent and summed in bfloat16 or wider, within the bound.
A program may use at most 64 MiB of HBM per device.

```python
import math
import jax
import jax.numpy as jnp
import numpy as np
from jax import lax

D = 2048
FF = 768
TOP = 8
TOK_DEV = 16
EXPERTS = 16
CAP = 16
SLOTS = 128
TOKENS = 256
N_DP = 2
N_EXPERT = 8
N_TENSOR = 2


def block_scale(stream_key, shape, pieces, low, largest):
    level = 1.0
    for axis_at, shards_of in pieces:
        draws = jax.random.uniform(jax.random.fold_in(jax.random.fold_in(stream_key, 6), axis_at), (shards_of,), jnp.float32, low / len(pieces), largest / len(pieces))
        level = level * jnp.repeat(jnp.exp(draws), shape[axis_at] // shards_of).reshape((-1,) + (1,) * (len(shape) - 1 - axis_at))
    return level


def routed_block(key, own, number, rows, number_of, top, limit, lean):
    order = jax.random.permutation(key, number_of)
    crowded, common = load_shares(number_of, rows * top, limit, lean, True), load_shares(number_of, rows * top, limit, lean, False)
    places = jnp.arange(number_of)

    def named(lengths, turn):
        used = int((lengths > 0).sum())
        fixed = max(1, used // 4)
        moved = fixed + (places - fixed + turn * (used - fixed)) % max(1, number_of - fixed)
        return jnp.zeros((number_of,), jnp.int32).at[order[jnp.where(places < fixed, places, moved)]].set(jnp.asarray(lengths, jnp.int32))

    lengths = jnp.where(number % 4 == 0, named(crowded, number // 4), named(common, number - number // 4 - 1))
    mixed = jax.random.permutation(jax.random.fold_in(own, 3), number_of)
    giver, receiver = mixed[0:number_of // 2 * 2:2], mixed[1:number_of // 2 * 2:2]
    margin = jnp.minimum(lengths[giver] - 1, limit - lengths[receiver]) // 2
    margin = jnp.where((giver == order[0]) | (receiver == order[0]) | (lengths[receiver] == 0), 0, jnp.maximum(margin, 0))
    moved = jax.random.randint(jax.random.fold_in(own, 4), (number_of // 2,), 0, 1 << 20) % (margin + 1)
    lengths = lengths.at[giver].add(-moved).at[receiver].add(moved)
    items = jnp.searchsorted(jnp.cumsum(lengths), jnp.arange(rows * top), side="right").astype(jnp.int32)
    table = items.reshape(top, rows).T
    table = table[jax.random.permutation(jax.random.fold_in(own, 1), rows)]
    turn = jax.random.randint(jax.random.fold_in(own, 2), (rows, 1), 0, top)
    return jnp.take_along_axis(table, (jnp.arange(top)[None, :] + turn) % top, axis=1)


def load_shares(count, total, most, skew, full):
    portions = [(1 << 20) // math.isqrt(standing ** skew) + 1 for standing in range(1, count + 1)]
    largest = most if full else min(most, max(-(-total // count), total * portions[0] // sum(portions)))
    least = 1 if total - largest >= count - 1 else 0
    holding, spare = [largest] + [least] * (count - 1), total - largest - least * (count - 1)
    while spare > 0:
        movable = [i for i in range(1, count) if holding[i] < largest] or [i for i in range(1, count) if holding[i] < most]
        whole, remaining = sum([portions[i] for i in movable]), spare
        for i in movable:
            more = min(most - holding[i], max(1, remaining * portions[i] // whole), spare)
            holding[i] = holding[i] + more
            spare = spare - more
    return np.array(holding)


def scatter_about(rng, dims, width, reach, cuts=(), kind=jnp.bfloat16):
    entries = jax.random.normal(rng, dims, jnp.float32) * width
    if len(cuts) > 0:
        entries = block_scale(rng, dims, cuts, -0.22, 0.18) * entries
    return jnp.clip(entries, min=-reach, max=reach).astype(kind)


def setup_inputs(seed: int = 0) -> dict:
    key_list = jax.random.split(jax.random.key(seed), 7)
    tokens = scatter_about(key_list[0], (TOKENS, D), 1.0, 6.0, ((0, 16),))
    routes_keys = jax.random.split(jax.random.fold_in(key_list[1], 1), TOKENS // TOK_DEV)
    routes_turns = jax.random.permutation(jax.random.fold_in(key_list[1], 3), TOKENS // TOK_DEV)
    routes = jax.vmap(lambda own, number: routed_block(jax.random.fold_in(key_list[1], 2), own, number, TOK_DEV, EXPERTS, TOP, CAP, 2))(routes_keys, routes_turns).reshape((TOKENS, TOP))
    route_weight = jnp.clip(jnp.exp(math.log(0.5) - 3.218876 * jax.random.uniform(key_list[2], (TOKENS, TOP), jnp.float32) ** block_scale(key_list[2], (TOKENS, TOP), ((0, 16),), -0.2, 0.2)), 0.02, 0.5)
    weights_gate_up = scatter_about(key_list[3], (EXPERTS, D, 2, FF), D ** -0.5, 0.125, ((0, 8), (3, 2)))
    weights_down = scatter_about(key_list[4], (EXPERTS, D, FF), FF ** -0.5, 0.21875, ((0, 8), (2, 2)))
    cotangent = scatter_about(key_list[5], (TOKENS, D), 1.0, 6.0, ((0, 16),))
    return dict(tokens=tokens, routes=routes, route_weight=route_weight, weights_gate_up=weights_gate_up, weights_down=weights_down, cotangent=cotangent)


def positions(routes):
    blocks = routes.reshape(-1, TOK_DEV * TOP)
    onehot = (blocks[:, :, None] == jnp.arange(EXPERTS, dtype=jnp.int32)[None, None, :]).astype(jnp.int32)
    earlier = jnp.cumsum(onehot, axis=1, dtype=jnp.int32) - onehot
    return jnp.sum(earlier * onehot, axis=2).astype(jnp.int32).reshape(-1)


def rounded(value):
    return lax.optimization_barrier(value.astype(jnp.bfloat16)).astype(jnp.float32)


def reference(tokens, routes, route_weight, weights_gate_up, weights_down, cotangent):
    hid_size = FF // N_TENSOR
    high = lax.Precision.HIGHEST
    expert_ids = routes.reshape(-1).astype(jnp.int32)
    row_ids = jnp.arange(TOKENS * TOP, dtype=jnp.int32)
    tok_ids = row_ids // TOP
    block_id = tok_ids // TOK_DEV
    group_id = block_id // N_EXPERT
    source_id = block_id % N_EXPERT
    slot_ids = source_id * CAP + positions(routes)
    empty = jnp.zeros((EXPERTS, N_DP, SLOTS, D), jnp.bfloat16)
    rows_in = empty.at[expert_ids, group_id, slot_ids].set(tokens[tok_ids])
    scaled = (route_weight.reshape(-1)[:, None] * cotangent[tok_ids].astype(jnp.float32)).astype(jnp.bfloat16)
    grads_in = empty.at[expert_ids, group_id, slot_ids].set(scaled)

    def per_expert(operands):
        rows_e, grads_e, w_gate_up, w_down = operands
        rows_f = rows_e.astype(jnp.float32)
        grads_f = grads_e.astype(jnp.float32)
        wgu_f = w_gate_up.astype(jnp.float32)
        wd_f = w_down.astype(jnp.float32)
        gate_up = jnp.einsum("gsd,dch->gsch", rows_f, wgu_f, precision=high)
        gate_pre = gate_up[:, :, 0, :]
        up_pre = gate_up[:, :, 1, :]
        sig_gate = jax.nn.sigmoid(gate_pre)
        silu_gate = gate_pre * sig_gate
        hidden = (silu_gate * up_pre).astype(jnp.bfloat16)
        hidden_f = hidden.astype(jnp.float32)
        out_part = jnp.einsum("gsqh,dqh->gsqd", hidden_f.reshape(N_DP, SLOTS, N_TENSOR, hid_size),
                              wd_f.reshape(D, N_TENSOR, hid_size), precision=high)
        expert_out = jnp.sum(rounded(out_part), axis=2).astype(jnp.bfloat16)
        hidden_grad = jnp.einsum("gsd,dh->gsh", grads_f, wd_f, precision=high)
        gate_grad = hidden_grad * up_pre * sig_gate * (1.0 + gate_pre * (1.0 - sig_gate))
        up_grad = hidden_grad * silu_gate
        pre_grads = jnp.stack([gate_grad, up_grad], axis=2).astype(jnp.bfloat16)
        pre_f = pre_grads.astype(jnp.float32)
        in_part = jnp.einsum("gscqh,dcqh->gsqd", pre_f.reshape(N_DP, SLOTS, 2, N_TENSOR, hid_size),
                             wgu_f.reshape(D, 2, N_TENSOR, hid_size), precision=high)
        expert_in_grad = jnp.sum(rounded(in_part), axis=2).astype(jnp.bfloat16)
        gu_terms = jnp.einsum("gsd,gsch->gdch", rows_f, pre_f, precision=high)
        gate_up_grad = jnp.sum(rounded(gu_terms), axis=0).astype(jnp.bfloat16)
        down_terms = jnp.einsum("gsd,gsh->gdh", grads_f, hidden_f, precision=high)
        down_grad = jnp.sum(rounded(down_terms), axis=0).astype(jnp.bfloat16)
        return expert_out, expert_in_grad, gate_up_grad, down_grad

    expert_out, expert_in_grad, gate_up_grad, down_grad = lax.map(
        per_expert, (rows_in, grads_in, weights_gate_up, weights_down))
    picked_out = expert_out[expert_ids, group_id, slot_ids].astype(jnp.float32).reshape(TOKENS, TOP, D)
    layer_out = jnp.sum(route_weight[:, :, None] * picked_out, axis=1).astype(jnp.bfloat16)
    picked_in = expert_in_grad[expert_ids, group_id, slot_ids].astype(jnp.float32).reshape(TOKENS, TOP, D)
    tokens_grad = jnp.sum(picked_in, axis=1).astype(jnp.bfloat16)
    return layer_out, tokens_grad, gate_up_grad, down_grad
```

```python
import jax
import jax.numpy as jnp
from jax import lax
from jax.sharding import PartitionSpec as P

F32 = jnp.float32
BF16 = jnp.bfloat16


def cut(value):
    return lax.reduce_precision(value, exponent_bits=8, mantissa_bits=7)


def body(tokens, routes, route_weight, weights_gate_up, weights_down, cotangent):
    tok_rows, width = tokens.shape
    expert_local = weights_gate_up.shape[0]
    n_expert = lax.axis_size("expert")
    n_tensor = lax.axis_size("tensor")
    n_dp = lax.axis_size("dp")
    expert_total = expert_local * n_expert
    group = tok_rows * n_expert
    my_dp = lax.axis_index("dp")

    chosen = routes[:, :, None] == jnp.arange(expert_total, dtype=jnp.int32)[None, None, :]
    dense = jnp.sum(jnp.where(chosen, route_weight[:, :, None], 0.0), axis=1)
    first = cut(dense)
    second = cut(dense - first)
    third = dense - first - second
    parts = jnp.concatenate([first, second, third], axis=1).astype(BF16)
    spare = -parts.shape[1] % 128
    parts = jnp.pad(parts, ((0, 0), (0, spare)))
    sent = jnp.concatenate([tokens, cotangent, parts], axis=1)
    held = lax.all_gather(sent, "expert", axis=0, tiled=True)
    tok = held[:, :width]
    cot = held[:, width : 2 * width]
    parts = held[:, 2 * width : 2 * width + 3 * expert_total].astype(F32)
    parts = parts.reshape(group, 3, expert_total)
    weight = parts[:, 0] + parts[:, 1] + parts[:, 2]
    weight = lax.dynamic_slice_in_dim(
        weight, lax.axis_index("expert") * expert_local, expert_local, axis=1
    ).T[:, :, None]

    share = width // n_dp

    def columns(shift):
        start = lax.rem(my_dp + shift, n_dp) * share
        return jnp.concatenate(
            [
                lax.dynamic_slice_in_dim(tok, start, share, axis=1),
                lax.dynamic_slice_in_dim(cot, start, share, axis=1),
            ],
            axis=1,
        )

    def moved(value, shift):
        return lax.ppermute(value, "dp", [(i, (i + shift) % n_dp) for i in range(n_dp)])

    sides = [columns(0)] + [moved(columns(s), s) for s in range(1, n_dp)]

    gate_up = jnp.einsum("td,edgh->etgh", tok, weights_gate_up, preferred_element_type=F32)
    gate_pre = gate_up[:, :, 0, :]
    up_pre = gate_up[:, :, 1, :]
    sig_gate = jax.nn.sigmoid(gate_pre)
    silu_gate = gate_pre * sig_gate
    hidden = (silu_gate * up_pre * weight).astype(BF16)
    hidden_grad = weight * jnp.einsum(
        "td,edh->eth", cot, weights_down, preferred_element_type=F32
    )
    gate_grad = (hidden_grad * up_pre * sig_gate * (1.0 + gate_pre * (1.0 - sig_gate))).astype(BF16)
    up_grad = (hidden_grad * silu_gate).astype(BF16)

    mine = jnp.stack([gate_grad, up_grad, hidden], axis=0)
    acts = jnp.concatenate([mine] + [moved(mine, s) for s in range(1, n_dp)], axis=2)

    pre_grads = jnp.stack([gate_grad, up_grad], axis=2)
    out_part = jnp.sum(
        jnp.einsum("eth,edh->etd", hidden, weights_down, preferred_element_type=F32), axis=0
    ).astype(BF16)
    in_part = jnp.sum(
        jnp.einsum("etgh,edgh->etd", pre_grads, weights_gate_up, preferred_element_type=F32),
        axis=0,
    ).astype(BF16)
    both = jnp.stack([out_part, in_part]).reshape(
        2, n_expert, tok_rows, n_tensor, width // n_tensor
    )
    both = both.transpose(1, 3, 0, 2, 4).reshape(
        n_expert * n_tensor, 2, tok_rows, width // n_tensor
    )
    back = lax.all_to_all(both, ("expert", "tensor"), split_axis=0, concat_axis=0, tiled=True)
    results = jnp.sum(back.astype(F32), axis=0).astype(BF16)

    rows = jnp.concatenate(sides, axis=0)
    gate_up_grad = jnp.einsum(
        "td,geth->edgh", rows[:, :share], acts[:2], preferred_element_type=F32
    ).astype(BF16)
    down_grad = jnp.einsum(
        "td,eth->edh", rows[:, share:], acts[2], preferred_element_type=F32
    ).astype(BF16)
    return results[0], results[1], gate_up_grad, down_grad


def solution(mesh):
    return jax.shard_map(
        body,
        mesh=mesh,
        in_specs=(
            P(("dp", "expert"), None),
            P(("dp", "expert"), None),
            P(("dp", "expert"), None),
            P("expert", None, None, "tensor"),
            P("expert", None, "tensor"),
            P(("dp", "expert"), None),
        ),
        out_specs=(
            P(("dp", "expert"), "tensor"),
            P(("dp", "expert"), "tensor"),
            P("expert", "dp", None, "tensor"),
            P("expert", "dp", "tensor"),
        ),
        check_vma=False,
    )
```

```python
import jax
import jax.numpy as jnp
from jax import lax
from jax.sharding import PartitionSpec as P

F32 = jnp.float32
BF16 = jnp.bfloat16


def cut(value):
    return lax.reduce_precision(value, exponent_bits=8, mantissa_bits=7)


def body(tokens, routes, route_weight, weights_gate_up, weights_down, cotangent):
    tok_rows, width = tokens.shape
    expert_local = weights_gate_up.shape[0]
    n_expert = lax.axis_size("expert")
    n_tensor = lax.axis_size("tensor")
    n_dp = lax.axis_size("dp")
    expert_total = expert_local * n_expert
    group = tok_rows * n_expert
    my_dp = lax.axis_index("dp")

    chosen = routes[:, :, None] == jnp.arange(expert_total, dtype=jnp.int32)[None, None, :]
    dense = jnp.sum(jnp.where(chosen, route_weight[:, :, None], 0.0), axis=1)
    first = cut(dense)
    second = cut(dense - first)
    third = dense - first - second
    parts = jnp.concatenate([first, second, third], axis=1).astype(BF16)
    spare = -parts.shape[1] % 128
    parts = jnp.pad(parts, ((0, 0), (0, spare)))
    sent = jnp.concatenate([tokens, cotangent, parts], axis=1)
    held = lax.all_gather(sent, "expert", axis=0, tiled=True)
    tok = held[:, :width]
    cot = held[:, width : 2 * width]
    parts = held[:, 2 * width : 2 * width + 3 * expert_total].astype(F32)
    parts = parts.reshape(group, 3, expert_total)
    weight = parts[:, 0] + parts[:, 1] + parts[:, 2]
    weight = lax.dynamic_slice_in_dim(
        weight, lax.axis_index("expert") * expert_local, expert_local, axis=1
    ).T[:, :, None]

    share = width // n_dp

    def columns(shift):
        start = lax.rem(my_dp + shift, n_dp) * share
        return jnp.concatenate(
            [
                lax.dynamic_slice_in_dim(tok, start, share, axis=1),
                lax.dynamic_slice_in_dim(cot, start, share, axis=1),
            ],
            axis=1,
        )

    def moved(value, shift):
        return lax.ppermute(value, "dp", [(i, (i + shift) % n_dp) for i in range(n_dp)])

    sides = [columns(0)] + [moved(columns(s), s) for s in range(1, n_dp)]

    gate_up = jnp.einsum("td,edgh->etgh", tok, weights_gate_up, preferred_element_type=F32)
    gate_pre = gate_up[:, :, 0, :]
    up_pre = gate_up[:, :, 1, :]
    sig_gate = jax.nn.sigmoid(gate_pre)
    silu_gate = gate_pre * sig_gate
    hidden = (silu_gate * up_pre * weight).astype(BF16)
    hidden_grad = weight * jnp.einsum(
        "td,edh->eth", cot, weights_down, preferred_element_type=F32
    )
    gate_grad = (hidden_grad * up_pre * sig_gate * (1.0 + gate_pre * (1.0 - sig_gate))).astype(BF16)
    up_grad = (hidden_grad * silu_gate).astype(BF16)

    pre_grads = jnp.stack([gate_grad, up_grad], axis=2)
    hidden_all = jnp.concatenate([hidden] + [moved(hidden, s) for s in range(1, n_dp)], axis=1)
    grads_all = jnp.concatenate([pre_grads] + [moved(pre_grads, s) for s in range(1, n_dp)], axis=1)
    out_part = jnp.sum(
        jnp.einsum("eth,edh->etd", hidden, weights_down, preferred_element_type=F32), axis=0
    ).astype(BF16)
    in_part = jnp.sum(
        jnp.einsum("etgh,edgh->etd", pre_grads, weights_gate_up, preferred_element_type=F32),
        axis=0,
    ).astype(BF16)
    both = jnp.stack([out_part, in_part]).reshape(
        2, n_expert, tok_rows, n_tensor, width // n_tensor
    )
    both = both.transpose(1, 3, 0, 2, 4).reshape(
        n_expert * n_tensor, 2, tok_rows, width // n_tensor
    )
    sides, both = lax.optimization_barrier((sides, both))
    back = lax.all_to_all(both, ("expert", "tensor"), split_axis=0, concat_axis=0, tiled=True)
    results = jnp.sum(back.astype(F32), axis=0).astype(BF16)

    rows = jnp.concatenate(sides, axis=0)
    gate_up_grad = jnp.einsum(
        "td,etgh->edgh", rows[:, :share], grads_all, preferred_element_type=F32
    ).astype(BF16)
    down_grad = jnp.einsum(
        "td,eth->edh", rows[:, share:], hidden_all, preferred_element_type=F32
    ).astype(BF16)
    return results[0], results[1], gate_up_grad, down_grad


def solution(mesh):
    return jax.shard_map(
        body,
        mesh=mesh,
        in_specs=(
            P(("dp", "expert"), None),
            P(("dp", "expert"), None),
            P(("dp", "expert"), None),
            P("expert", None, None, "tensor"),
            P("expert", None, "tensor"),
            P(("dp", "expert"), None),
        ),
        out_specs=(
            P(("dp", "expert"), "tensor"),
            P(("dp", "expert"), "tensor"),
            P("expert", "dp", None, "tensor"),
            P("expert", "dp", "tensor"),
        ),
        check_vma=False,
    )
```

```python
import jax
import jax.numpy as jnp
from jax import lax
from jax.sharding import PartitionSpec as P

F32 = jnp.float32
BF16 = jnp.bfloat16


def cut(value):
    return lax.reduce_precision(value, exponent_bits=8, mantissa_bits=7)


def body(tokens, routes, route_weight, weights_gate_up, weights_down, cotangent):
    tok_rows, width = tokens.shape
    expert_local = weights_gate_up.shape[0]
    n_expert = lax.axis_size("expert")
    n_tensor = lax.axis_size("tensor")
    n_dp = lax.axis_size("dp")
    expert_total = expert_local * n_expert
    group = tok_rows * n_expert
    my_dp = lax.axis_index("dp")

    chosen = routes[:, :, None] == jnp.arange(expert_total, dtype=jnp.int32)[None, None, :]
    dense = jnp.sum(jnp.where(chosen, route_weight[:, :, None], 0.0), axis=1)
    first = cut(dense)
    second = cut(dense - first)
    third = dense - first - second
    parts = jnp.concatenate([first, second, third], axis=1).astype(BF16)
    spare = -parts.shape[1] % 128
    parts = jnp.pad(parts, ((0, 0), (0, spare)))
    sent = jnp.concatenate([tokens, cotangent, parts], axis=1)
    held = lax.all_gather(sent, "expert", axis=0, tiled=True)
    tok = held[:, :width]
    cot = held[:, width : 2 * width]
    parts = held[:, 2 * width : 2 * width + 3 * expert_total].astype(F32)
    parts = parts.reshape(group, 3, expert_total)
    weight = parts[:, 0] + parts[:, 1] + parts[:, 2]
    weight = lax.dynamic_slice_in_dim(
        weight, lax.axis_index("expert") * expert_local, expert_local, axis=1
    ).T[:, :, None]

    share = width // n_dp

    def columns(shift):
        start = lax.rem(my_dp + shift, n_dp) * share
        return jnp.concatenate(
            [
                lax.dynamic_slice_in_dim(tok, start, share, axis=1),
                lax.dynamic_slice_in_dim(cot, start, share, axis=1),
            ],
            axis=1,
        )

    def moved(value, shift):
        return lax.ppermute(value, "dp", [(i, (i + shift) % n_dp) for i in range(n_dp)])

    sides = [columns(0)] + [moved(columns(s), s) for s in range(1, n_dp)]

    gate_up = jnp.einsum("td,edgh->etgh", tok, weights_gate_up, preferred_element_type=F32)
    gate_pre = gate_up[:, :, 0, :]
    up_pre = gate_up[:, :, 1, :]
    sig_gate = jax.nn.sigmoid(gate_pre)
    silu_gate = gate_pre * sig_gate
    hidden = (silu_gate * up_pre * weight).astype(BF16)
    hidden_grad = weight * jnp.einsum(
        "td,edh->eth", cot, weights_down, preferred_element_type=F32
    )
    gate_grad = (hidden_grad * up_pre * sig_gate * (1.0 + gate_pre * (1.0 - sig_gate))).astype(BF16)
    up_grad = (hidden_grad * silu_gate).astype(BF16)

    pre_grads = jnp.stack([gate_grad, up_grad], axis=2)
    hidden_all = jnp.concatenate([hidden] + [moved(hidden, s) for s in range(1, n_dp)], axis=1)
    grads_all = jnp.concatenate([pre_grads] + [moved(pre_grads, s) for s in range(1, n_dp)], axis=1)
    out_part = jnp.sum(
        jnp.einsum("eth,edh->etd", hidden, weights_down, preferred_element_type=F32), axis=0
    ).astype(BF16)
    in_part = jnp.sum(
        jnp.einsum("etgh,edgh->etd", pre_grads, weights_gate_up, preferred_element_type=F32),
        axis=0,
    ).astype(BF16)
    both = jnp.stack([out_part, in_part]).reshape(
        2, n_expert, tok_rows, n_tensor, width // n_tensor
    )
    both = both.transpose(1, 3, 0, 2, 4).reshape(
        n_expert * n_tensor, 2, tok_rows, width // n_tensor
    )
    sides, hidden_all, grads_all, both = lax.optimization_barrier(
        (sides, hidden_all, grads_all, both)
    )
    back = lax.all_to_all(both, ("expert", "tensor"), split_axis=0, concat_axis=0, tiled=True)
    results = jnp.sum(back.astype(F32), axis=0).astype(BF16)

    rows = jnp.concatenate(sides, axis=0)
    gate_up_grad = jnp.einsum(
        "td,etgh->edgh", rows[:, :share], grads_all, preferred_element_type=F32
    ).astype(BF16)
    down_grad = jnp.einsum(
        "td,eth->edh", rows[:, share:], hidden_all, preferred_element_type=F32
    ).astype(BF16)
    return results[0], results[1], gate_up_grad, down_grad


def solution(mesh):
    return jax.shard_map(
        body,
        mesh=mesh,
        in_specs=(
            P(("dp", "expert"), None),
            P(("dp", "expert"), None),
            P(("dp", "expert"), None),
            P("expert", None, None, "tensor"),
            P("expert", None, "tensor"),
            P(("dp", "expert"), None),
        ),
        out_specs=(
            P(("dp", "expert"), "tensor"),
            P(("dp", "expert"), "tensor"),
            P("expert", "dp", None, "tensor"),
            P("expert", "dp", "tensor"),
        ),
        check_vma=False,
    )
```

```python
import functools

import jax
import jax.numpy as jnp
from jax import lax
from jax.experimental import pallas as pl
from jax.experimental.pallas import tpu as pltpu
from jax.sharding import PartitionSpec as P

F32 = jnp.float32
BF16 = jnp.bfloat16


def cut(value):
    return lax.reduce_precision(value, exponent_bits=8, mantissa_bits=7)


def gradient_kernel(n, width, *refs):
    tok_refs, cot_refs, act_refs = refs[:n], refs[n : 2 * n], refs[2 * n : 3 * n]
    gate_up_ref, down_ref, mixed = refs[3 * n :]
    tok = jnp.concatenate([r[...] for r in tok_refs], axis=0)
    cot = jnp.concatenate([r[...] for r in cot_refs], axis=0)
    acts = jnp.concatenate([r[0] for r in act_refs], axis=0)
    over_tokens = (((0,), (0,)), ((), ()))
    gate_up = lax.dot_general(
        tok, acts[:, : 2 * width], over_tokens, preferred_element_type=F32
    )
    down = lax.dot_general(cot, acts[:, 2 * width :], over_tokens, preferred_element_type=F32)
    down_ref[0] = down.astype(BF16)
    halves = [gate_up[:, g * width : (g + 1) * width] for g in range(2)]
    gate_up_ref[0] = jnp.stack(halves, axis=1).astype(BF16)


def gradients(sides, acts, share):
    n = len(sides)
    experts, tokens, width = acts[0].shape
    width //= 3
    rows = 256
    steps = share // rows
    gate_up, down = pl.pallas_call(
        functools.partial(gradient_kernel, n, width),
        grid=(experts, steps),
        in_specs=[pl.BlockSpec((tokens, rows), lambda e, j: (0, j))] * n
        + [pl.BlockSpec((tokens, rows), lambda e, j: (0, steps + j))] * n
        + [pl.BlockSpec((1, tokens, 3 * width), lambda e, j: (e, 0, 0))] * n,
        out_specs=[
            pl.BlockSpec((1, rows, 2, width), lambda e, j: (e, j, 0, 0)),
            pl.BlockSpec((1, rows, width), lambda e, j: (e, j, 0)),
        ],
        out_shape=[
            jax.ShapeDtypeStruct((experts, share, 2, width), BF16),
            jax.ShapeDtypeStruct((experts, share, width), BF16),
        ],
        scratch_shapes=[pltpu.VMEM((rows, 2, width), F32)],
        compiler_params=pltpu.CompilerParams(vmem_limit_bytes=24 * 1024 * 1024),
        cost_estimate=pl.CostEstimate(
            flops=6 * n * experts * tokens * share * width,
            bytes_accessed=6 * experts * share * width + 8 * n * tokens * share,
            transcendentals=0,
        ),
    )(*sides, *sides, *acts)
    return gate_up, down


def body(tokens, routes, route_weight, weights_gate_up, weights_down, cotangent):
    tok_rows, width = tokens.shape
    expert_local = weights_gate_up.shape[0]
    n_expert = lax.axis_size("expert")
    n_tensor = lax.axis_size("tensor")
    n_dp = lax.axis_size("dp")
    expert_total = expert_local * n_expert
    group = tok_rows * n_expert
    my_dp = lax.axis_index("dp")

    chosen = routes[:, :, None] == jnp.arange(expert_total, dtype=jnp.int32)[None, None, :]
    dense = jnp.sum(jnp.where(chosen, route_weight[:, :, None], 0.0), axis=1)
    first = cut(dense)
    second = cut(dense - first)
    third = dense - first - second
    parts = jnp.concatenate([first, second, third], axis=1).astype(BF16)
    spare = -parts.shape[1] % 128
    parts = jnp.pad(parts, ((0, 0), (0, spare)))
    sent = jnp.concatenate([tokens, cotangent, parts], axis=1)
    held = lax.all_gather(sent, "expert", axis=0, tiled=True)
    tok = held[:, :width]
    cot = held[:, width : 2 * width]
    parts = held[:, 2 * width : 2 * width + 3 * expert_total].astype(F32)
    parts = parts.reshape(group, 3, expert_total)
    weight = parts[:, 0] + parts[:, 1] + parts[:, 2]
    weight = lax.dynamic_slice_in_dim(
        weight, lax.axis_index("expert") * expert_local, expert_local, axis=1
    ).T[:, :, None]

    share = width // n_dp

    def columns(shift):
        start = lax.rem(my_dp + shift, n_dp) * share
        return jnp.concatenate(
            [
                lax.dynamic_slice_in_dim(tok, start, share, axis=1),
                lax.dynamic_slice_in_dim(cot, start, share, axis=1),
            ],
            axis=1,
        )

    def moved(value, shift):
        return lax.ppermute(value, "dp", [(i, (i + shift) % n_dp) for i in range(n_dp)])

    sides = [columns(0)] + [moved(columns(s), s) for s in range(1, n_dp)]

    gate_up = jnp.einsum("td,edgh->etgh", tok, weights_gate_up, preferred_element_type=F32)
    gate_pre = gate_up[:, :, 0, :]
    up_pre = gate_up[:, :, 1, :]
    sig_gate = jax.nn.sigmoid(gate_pre)
    silu_gate = gate_pre * sig_gate
    hidden = (silu_gate * up_pre * weight).astype(BF16)
    hidden_grad = weight * jnp.einsum(
        "td,edh->eth", cot, weights_down, preferred_element_type=F32
    )
    gate_grad = (hidden_grad * up_pre * sig_gate * (1.0 + gate_pre * (1.0 - sig_gate))).astype(BF16)
    up_grad = (hidden_grad * silu_gate).astype(BF16)

    pre_grads = jnp.stack([gate_grad, up_grad], axis=2)
    mine = jnp.concatenate([gate_grad, up_grad, hidden], axis=2)
    acts = [mine] + [moved(mine, s) for s in range(1, n_dp)]
    sides, hidden, pre_grads = lax.optimization_barrier((sides, hidden, pre_grads))
    out_part = jnp.sum(
        jnp.einsum("eth,edh->etd", hidden, weights_down, preferred_element_type=F32), axis=0
    ).astype(BF16)
    in_part = jnp.sum(
        jnp.einsum("etgh,edgh->etd", pre_grads, weights_gate_up, preferred_element_type=F32),
        axis=0,
    ).astype(BF16)
    part = width // n_tensor
    slabs = [
        value[:, i * part : (i + 1) * part].reshape(n_expert, tok_rows, part)
        for i in range(n_tensor)
        for value in (out_part, in_part)
    ]
    both = jnp.stack(slabs, axis=1).reshape(n_expert * n_tensor, 2, tok_rows, part)
    back = lax.all_to_all(both, ("expert", "tensor"), split_axis=0, concat_axis=0, tiled=True)
    results = jnp.sum(back.astype(F32), axis=0).astype(BF16)

    wide = hidden.shape[2]
    if wide % 128 == 0 and share % 256 == 0 and group % 16 == 0:
        gate_up_grad, down_grad = gradients(sides, acts, share)
    else:
        rows = jnp.concatenate(sides, axis=0)
        acts = jnp.concatenate(acts, axis=1)
        gate_up_grad = jnp.einsum(
            "td,etgh->edgh",
            rows[:, :share],
            acts[:, :, : 2 * wide].reshape(*acts.shape[:2], 2, wide),
            preferred_element_type=F32,
        ).astype(BF16)
        down_grad = jnp.einsum(
            "td,eth->edh", rows[:, share:], acts[:, :, 2 * wide :], preferred_element_type=F32
        ).astype(BF16)
    return results[0], results[1], gate_up_grad, down_grad


def solution(mesh):
    return jax.shard_map(
        body,
        mesh=mesh,
        in_specs=(
            P(("dp", "expert"), None),
            P(("dp", "expert"), None),
            P(("dp", "expert"), None),
            P("expert", None, None, "tensor"),
            P("expert", None, "tensor"),
            P(("dp", "expert"), None),
        ),
        out_specs=(
            P(("dp", "expert"), "tensor"),
            P(("dp", "expert"), "tensor"),
            P("expert", "dp", None, "tensor"),
            P("expert", "dp", "tensor"),
        ),
        check_vma=False,
    )
```

```python
import functools

import jax
import jax.numpy as jnp
from jax import lax
from jax.experimental import pallas as pl
from jax.experimental.pallas import tpu as pltpu
from jax.sharding import PartitionSpec as P

F32 = jnp.float32
BF16 = jnp.bfloat16


def cut(value):
    return lax.reduce_precision(value, exponent_bits=8, mantissa_bits=7)


def gradient_kernel(n, width, *refs):
    tok_refs, cot_refs, act_refs = refs[:n], refs[n : 2 * n], refs[2 * n : 3 * n]
    gate_up_ref, down_ref, mixed = refs[3 * n :]
    tok = jnp.concatenate([r[...] for r in tok_refs], axis=0)
    cot = jnp.concatenate([r[...] for r in cot_refs], axis=0)
    acts = jnp.concatenate([r[0] for r in act_refs], axis=0)
    over_tokens = (((0,), (0,)), ((), ()))
    gate_up = lax.dot_general(
        tok, acts[:, : 2 * width], over_tokens, preferred_element_type=F32
    )
    down = lax.dot_general(cot, acts[:, 2 * width :], over_tokens, preferred_element_type=F32)
    down_ref[0] = down.astype(BF16)
    halves = [gate_up[:, g * width : (g + 1) * width] for g in range(2)]
    gate_up_ref[0] = jnp.stack(halves, axis=1).astype(BF16)


def gradients(toks, cots, acts, share):
    n = len(toks)
    experts, tokens, width = acts[0].shape
    width //= 3
    rows = 256
    steps = share // rows
    gate_up, down = pl.pallas_call(
        functools.partial(gradient_kernel, n, width),
        grid=(experts, steps),
        in_specs=[pl.BlockSpec((tokens, rows), lambda e, j: (0, j))] * n
        + [pl.BlockSpec((tokens, rows), lambda e, j: (0, j))] * n
        + [pl.BlockSpec((1, tokens, 3 * width), lambda e, j: (e, 0, 0))] * n,
        out_specs=[
            pl.BlockSpec((1, rows, 2, width), lambda e, j: (e, j, 0, 0)),
            pl.BlockSpec((1, rows, width), lambda e, j: (e, j, 0)),
        ],
        out_shape=[
            jax.ShapeDtypeStruct((experts, share, 2, width), BF16),
            jax.ShapeDtypeStruct((experts, share, width), BF16),
        ],
        scratch_shapes=[pltpu.VMEM((rows, 2, width), F32)],
        compiler_params=pltpu.CompilerParams(vmem_limit_bytes=24 * 1024 * 1024),
        cost_estimate=pl.CostEstimate(
            flops=6 * n * experts * tokens * share * width,
            bytes_accessed=6 * experts * share * width + 8 * n * tokens * share,
            transcendentals=0,
        ),
    )(*toks, *cots, *acts)
    return gate_up, down


def body(tokens, routes, route_weight, weights_gate_up, weights_down, cotangent):
    tok_rows, width = tokens.shape
    expert_local = weights_gate_up.shape[0]
    n_expert = lax.axis_size("expert")
    n_tensor = lax.axis_size("tensor")
    n_dp = lax.axis_size("dp")
    expert_total = expert_local * n_expert
    group = tok_rows * n_expert
    my_dp = lax.axis_index("dp")

    chosen = routes[:, :, None] == jnp.arange(expert_total, dtype=jnp.int32)[None, None, :]
    dense = jnp.sum(jnp.where(chosen, route_weight[:, :, None], 0.0), axis=1)
    first = cut(dense)
    second = cut(dense - first)
    third = dense - first - second
    parts = jnp.concatenate([first, second, third], axis=1).astype(BF16)
    spare = -parts.shape[1] % 128
    parts = jnp.pad(parts, ((0, 0), (0, spare)))
    sent = jnp.concatenate([tokens, cotangent, parts], axis=1)
    held = lax.all_gather(sent, "expert", axis=0, tiled=True)
    tok = held[:, :width]
    cot = held[:, width : 2 * width]
    parts = held[:, 2 * width : 2 * width + 3 * expert_total].astype(F32)
    parts = parts.reshape(group, 3, expert_total)
    weight = parts[:, 0] + parts[:, 1] + parts[:, 2]
    weight = lax.dynamic_slice_in_dim(
        weight, lax.axis_index("expert") * expert_local, expert_local, axis=1
    ).T[:, :, None]

    share = width // n_dp

    def columns(value, shift):
        start = lax.rem(my_dp + shift, n_dp) * share
        return lax.dynamic_slice_in_dim(value, start, share, axis=1)

    def moved(value, shift):
        return lax.ppermute(value, "dp", [(i, (i + shift) % n_dp) for i in range(n_dp)])

    toks = [columns(tok, 0)] + [moved(columns(tok, s), s) for s in range(1, n_dp)]
    cots = [columns(cot, 0)] + [moved(columns(cot, s), s) for s in range(1, n_dp)]

    gate_up = jnp.einsum("td,edgh->etgh", tok, weights_gate_up, preferred_element_type=F32)
    gate_pre = gate_up[:, :, 0, :]
    up_pre = gate_up[:, :, 1, :]
    sig_gate = jax.nn.sigmoid(gate_pre)
    silu_gate = gate_pre * sig_gate
    hidden = (silu_gate * up_pre * weight).astype(BF16)
    hidden_grad = weight * jnp.einsum(
        "td,edh->eth", cot, weights_down, preferred_element_type=F32
    )
    gate_grad = (hidden_grad * up_pre * sig_gate * (1.0 + gate_pre * (1.0 - sig_gate))).astype(BF16)
    up_grad = (hidden_grad * silu_gate).astype(BF16)

    pre_grads = jnp.stack([gate_grad, up_grad], axis=2)
    mine = jnp.concatenate([gate_grad, up_grad, hidden], axis=2)
    acts = [mine] + [moved(mine, s) for s in range(1, n_dp)]
    toks, hidden, pre_grads = lax.optimization_barrier((toks, hidden, pre_grads))
    out_part = jnp.sum(
        jnp.einsum("eth,edh->etd", hidden, weights_down, preferred_element_type=F32), axis=0
    ).astype(BF16)
    in_part = jnp.sum(
        jnp.einsum("etgh,edgh->etd", pre_grads, weights_gate_up, preferred_element_type=F32),
        axis=0,
    ).astype(BF16)
    cots, in_part = lax.optimization_barrier((cots, in_part))
    part = width // n_tensor
    slabs = [
        value[:, i * part : (i + 1) * part].reshape(n_expert, tok_rows, part)
        for i in range(n_tensor)
        for value in (out_part, in_part)
    ]
    both = jnp.stack(slabs, axis=1).reshape(n_expert * n_tensor, 2, tok_rows, part)
    back = lax.all_to_all(both, ("expert", "tensor"), split_axis=0, concat_axis=0, tiled=True)
    results = jnp.sum(back.astype(F32), axis=0).astype(BF16)

    wide = hidden.shape[2]
    if wide % 128 == 0 and share % 256 == 0 and group % 16 == 0:
        gate_up_grad, down_grad = gradients(toks, cots, acts, share)
    else:
        acts = jnp.concatenate(acts, axis=1)
        gate_up_grad = jnp.einsum(
            "td,etgh->edgh",
            jnp.concatenate(toks, axis=0),
            acts[:, :, : 2 * wide].reshape(*acts.shape[:2], 2, wide),
            preferred_element_type=F32,
        ).astype(BF16)
        down_grad = jnp.einsum(
            "td,eth->edh", jnp.concatenate(cots, axis=0), acts[:, :, 2 * wide :], preferred_element_type=F32
        ).astype(BF16)
    return results[0], results[1], gate_up_grad, down_grad


def solution(mesh):
    return jax.shard_map(
        body,
        mesh=mesh,
        in_specs=(
            P(("dp", "expert"), None),
            P(("dp", "expert"), None),
            P(("dp", "expert"), None),
            P("expert", None, None, "tensor"),
            P("expert", None, "tensor"),
            P(("dp", "expert"), None),
        ),
        out_specs=(
            P(("dp", "expert"), "tensor"),
            P(("dp", "expert"), "tensor"),
            P("expert", "dp", None, "tensor"),
            P("expert", "dp", "tensor"),
        ),
        check_vma=False,
    )
```
